32 devices in a mesh: seq: 8 (over z, y), head: 4 (over x, core).
Axes of the slice: x: 2, y: 2, z: 4, core: 2. Of those that a mesh axis runs over, the one named last changes fastest.
Arguments:
- queries: bfloat16 [1024, 2048], P('seq', 'head'), may hold values from -6 to 6
- keys: bfloat16 [1024, 2048], P('seq', 'head'), may hold values from -6 to 6
- values: bfloat16 [1024, 2048], P('seq', 'head'), may hold values from -6 to 6
- grad_out: bfloat16 [1024, 2048], P('seq', 'head'), may hold values from -6 to 6
- gain: float32 [2048], P('head'), may hold values from 0.1 to 1.9
- segment_ids: int32 [8, 128], P('seq'), may hold values from 0 to 7, never falling along the last dimension, each value on 1 to 32 neighbouring positions
Outputs:
- output: bfloat16 [1024, 2048], P('seq', 'head')
- grad_queries: bfloat16 [1024, 2048], P('seq', 'head')
- grad_keys: bfloat16 [1024, 2048], P('seq', 'head')
- grad_values: bfloat16 [1024, 2048], P('seq', 'head')
The draws below stay inside these ranges and needn't reach their ends.
Inputs may be any that keep to these rules, and one draw needn't show every extreme that they name: `segment_ids`: ids never fall along a group; each mask block holds 1 to 32 tokens, one exactly 32.
All inputs are finite; a program needn't handle non-finite values.
Results may differ from the reference program's by a relative error of at most 0.0058.
Values sent between devices are 32-bit elements; how exact they have to be, the bound alone decides.
A program may use at most 64 MiB of HBM per device.

```python
import math
import jax
import jax.numpy as jnp
import numpy as np
from jax import lax

HEADS = 16
HD = 128
D = 2048
TOK_DEV = 128
SEG_COUNT = 8
SEG_MOST = 32
GROUPS = 8
TOKENS = 1024


def steps_of(rng, dims, split, low, largest):
    level = 1.0
    for dim, parts in split:
        steps = jax.random.uniform(jax.random.fold_in(jax.random.fold_in(rng, 6), dim), (parts,), jnp.float32, low / len(split), largest / len(split))
        level = level * jnp.repeat(jnp.exp(steps), dims[dim] // parts).reshape((-1,) + (1,) * (len(dims) - 1 - dim))
    return level


def profile(number_of, total, bound, lean):
    loads = [(1 << 20) // math.isqrt(grade ** lean) + 1 for grade in range(2, number_of + 1)]
    rest, holding = total - bound - (number_of - 1), [1] * (number_of - 1)
    while rest > 0:
        candidates = [i for i in range(number_of - 1) if holding[i] < bound]
        pool, left = sum([loads[i] for i in candidates]), rest
        for i in candidates:
            more = min(bound - holding[i], max(1, left * loads[i] // pool), rest)
            holding[i] = holding[i] + more
            rest = rest - more
    return np.array([bound] + holding)


def uneven_parts(stream_key, count, total, most, lean):
    if count == 2:
        one = jax.random.randint(stream_key, (), max(1, total - most), min(most, total - 1) + 1)
        return jnp.stack([one, total - one])
    sizes = jnp.asarray(profile(count, total, most, lean), jnp.int32)
    twos = (count - 1) // 2
    giver, taker = sizes[1:1 + 2 * twos:2], sizes[2:2 + 2 * twos:2]
    slack = jnp.minimum(giver - 1, most - taker)
    passed = jax.random.randint(jax.random.fold_in(stream_key, 1), (twos,), 0, 1 << 20) % (slack + 1)
    sizes = sizes.at[1:1 + 2 * twos:2].set(giver - passed).at[2:2 + 2 * twos:2].set(taker + passed)
    return sizes[jax.random.permutation(jax.random.fold_in(stream_key, 2), count)]


def bell_draw(rng, extent, spread, most, pieces=(), held_as=jnp.bfloat16):
    values = jax.random.normal(rng, extent, jnp.float32) * spread
    if len(pieces) > 0:
        values = steps_of(rng, extent, pieces, -0.22, 0.18) * values
    return jnp.clip(values, min=-most, max=most).astype(held_as)


def setup_inputs(seed: int = 0) -> dict:
    streams_of = jax.random.split(jax.random.key(seed), 7)
    queries = bell_draw(streams_of[0], (TOKENS, D), 1.0, 6.0, ((0, 8), (1, 4)))
    keys = bell_draw(streams_of[1], (TOKENS, D), 1.0, 6.0, ((0, 8), (1, 4)))
    values = bell_draw(streams_of[2], (TOKENS, D), 1.0, 6.0, ((0, 8), (1, 4)))
    grad_out = bell_draw(streams_of[3], (TOKENS, D), 1.0, 6.0, ((0, 8), (1, 4)))
    gain = jnp.clip(1.0 + 0.18 * jax.random.normal(streams_of[4], (D,), jnp.float32), 0.1, 1.9)
    segment_ids = jax.vmap(lambda own: jnp.searchsorted(jnp.cumsum(uneven_parts(own, SEG_COUNT, TOK_DEV, SEG_MOST, 2)), jnp.arange(TOK_DEV), side="right"))(jax.random.split(streams_of[5], GROUPS)).reshape((GROUPS, TOK_DEV)).astype(jnp.int32)
    return dict(queries=queries, keys=keys, values=values, grad_out=grad_out, gain=gain, segment_ids=segment_ids)


def rounded(x):
    return lax.optimization_barrier(x.astype(jnp.bfloat16)).astype(jnp.float32)

def block_mask(segment):
    row_ids = lax.broadcasted_iota(jnp.int32, (TOK_DEV, TOK_DEV), 0)
    col_ids = lax.broadcasted_iota(jnp.int32, (TOK_DEV, TOK_DEV), 1)
    same = segment[:, None] == segment[None, :]
    return jnp.where(same & (col_ids <= row_ids), 1.0, 0.0).astype(jnp.float32)

def reference(queries, keys, values, grad_out, gain, segment_ids):
    shape4 = (GROUPS, TOK_DEV, HEADS, HD)
    q_all = queries.reshape(shape4)
    k_all = keys.reshape(shape4)
    v_all = values.reshape(shape4)
    dy_all = grad_out.reshape(GROUPS, TOK_DEV, D)
    gain_f = gain.astype(jnp.float32)

    def forward(carry, inputs):
        q_c, k_c, v_c, dy_c, segment = inputs
        allowed = block_mask(segment)
        q_f = q_c.astype(jnp.float32)
        k_f = k_c.astype(jnp.float32)
        v_f = v_c.astype(jnp.float32)
        scores = rounded(jnp.einsum('thd,shd->hts', q_f, k_f) * allowed[None])
        attn = jnp.einsum('hts,she->the', scores, v_f) + jnp.einsum('thd,hde->the', q_f, rounded(carry))
        flat = attn.reshape(TOK_DEV, D)
        inverse = lax.rsqrt(lax.optimization_barrier(jnp.sum(flat * flat, axis=1)) / D + 1e-06)
        out_c = (gain_f * flat * inverse[:, None]).astype(jnp.bfloat16)
        gained = gain_f * dy_c.astype(jnp.float32)
        products = lax.optimization_barrier(jnp.sum(gained * flat, axis=1))
        dflat = gained * inverse[:, None] - flat * (products * inverse ** 3 / D)[:, None]
        dattn = dflat.astype(jnp.bfloat16)
        dattn_f = dattn.astype(jnp.float32).reshape(TOK_DEV, HEADS, HD)
        grad_local = jnp.einsum('thd,the->hde', q_f, dattn_f)
        new_carry = carry + jnp.einsum('thd,the->hde', k_f, v_f)
        return (new_carry, (out_c, dattn, carry, grad_local))
    start = jnp.zeros((HEADS, HD, HD), jnp.float32)
    ignored, (outs, dattns, states, grads) = lax.scan(forward, start, (q_all, k_all, v_all, dy_all, segment_ids))

    def backward_sum(carry, grad_local):
        return (carry + grad_local, carry)
    ignored2, laters = lax.scan(backward_sum, start, grads, reverse=True)

    def backward(inputs):
        q_c, k_c, v_c, dattn, segment, state, later = inputs
        allowed = block_mask(segment)
        q_f = q_c.astype(jnp.float32)
        k_f = k_c.astype(jnp.float32)
        v_f = v_c.astype(jnp.float32)
        dattn_f = dattn.astype(jnp.float32).reshape(TOK_DEV, HEADS, HD)
        scores = rounded(jnp.einsum('thd,shd->hts', q_f, k_f) * allowed[None])
        dscores = rounded(jnp.einsum('the,she->hts', dattn_f, v_f) * allowed[None])
        state_b = rounded(state)
        later_b = rounded(later)
        grad_q = jnp.einsum('hts,shd->thd', dscores, k_f) + jnp.einsum('the,hde->thd', dattn_f, state_b)
        grad_k = jnp.einsum('hts,thd->shd', dscores, q_f) + jnp.einsum('she,hde->shd', v_f, later_b)
        grad_v = jnp.einsum('hts,the->she', scores, dattn_f) + jnp.einsum('shd,hde->she', k_f, later_b)
        return (grad_q.reshape(TOK_DEV, D).astype(jnp.bfloat16), grad_k.reshape(TOK_DEV, D).astype(jnp.bfloat16), grad_v.reshape(TOK_DEV, D).astype(jnp.bfloat16))
    grad_q, grad_k, grad_v = lax.map(backward, (q_all, k_all, v_all, dattns, segment_ids, states, laters))
    return (outs.reshape(TOKENS, D), grad_q.reshape(TOKENS, D), grad_k.reshape(TOKENS, D), grad_v.reshape(TOKENS, D))
```

```python
import functools

import jax
import jax.numpy as jnp
from jax import lax
from jax.experimental import pallas as pl
from jax.experimental.pallas import tpu as pltpu
from jax.sharding import PartitionSpec as P

HD = 128
INNER = 2
PARTS = 2
MESH = pl.DeviceIdType.MESH
F32 = jnp.float32
BF16 = jnp.bfloat16


def dot(a, b, dims):
    return lax.dot_general(a, b, (dims, ((), ())), preferred_element_type=F32)


NN = ((1,), (0,))
NT = ((1,), (1,))
TN = ((0,), (0,))


def kernel(
    n_seq, n_head, heads, q_ref, k_ref, v_ref, dy_ref, gain_ref, seg_ref,
    out_ref, gq_ref, gk_ref, gv_ref,
    own, zin, yin, scores, state_b, attn, dattn, part_k, part_v, norm_out, norm_in,
    zs, zr, ys, yr, ns, nr,
):
    length = q_ref.shape[0]
    features = n_head * heads * HD
    rows = HD // PARTS
    chunks = heads * PARTS
    s, h = lax.axis_index("seq"), lax.axis_index("head")
    y, z = lax.rem(s, INNER), s // INNER
    depth = n_seq // INNER
    across = s + 1 - 2 * y
    bottom, top = z == 0, z == depth - 1
    inner = jnp.logical_not(bottom), jnp.logical_not(top)

    def cols(i):
        return slice(i * HD, (i + 1) * HD)

    def peer(k):
        return lax.rem(h + k, n_head)

    barrier = pltpu.get_barrier_semaphore()
    pl.semaphore_signal(barrier, inc=1, device_id=(across, h), device_id_type=MESH)
    for k in range(1, n_head):
        pl.semaphore_signal(barrier, inc=1, device_id=(s, peer(k)), device_id_type=MESH)

    @pl.when(inner[0])
    def _():
        pl.semaphore_signal(barrier, inc=1, device_id=(s - INNER, h), device_id_type=MESH)

    @pl.when(inner[1])
    def _():
        pl.semaphore_signal(barrier, inc=1, device_id=(s + INNER, h), device_id_type=MESH)

    starts = (bottom, top)
    ends = (top, bottom)
    nexts = (s + INNER, s - INNER)
    gives_all = (y == 0, y == 1)

    def hop(p, c):
        return pltpu.make_async_remote_copy(
            src_ref=own.at[p, c], dst_ref=zin.at[p, c], send_sem=zs.at[p, c],
            recv_sem=zr.at[p, c], device_id=(nexts[p], h), device_id_type=MESH,
        )

    def cross(p, c, src):
        return pltpu.make_async_remote_copy(
            src_ref=src.at[p, c], dst_ref=yin.at[p, c], send_sem=ys.at[p, c],
            recv_sem=yr.at[p, c], device_id=(across, h), device_id_type=MESH,
        )

    def keep(p, i, term):
        for j in range(PARTS):
            own[p, i * PARTS + j] = term[j * rows:(j + 1) * rows]

    def send_first(p):
        @pl.when(starts[p])
        def _():
            for c in range(chunks):
                hop(p, c).start()

                @pl.when(gives_all[p])
                def _():
                    cross(p, c, own).start()

    def clear(p):
        @pl.when(starts[p])
        def _():
            zin[p] = jnp.zeros(zin.shape[1:], F32)

            @pl.when(gives_all[p])
            def _():
                yin[p] = jnp.zeros(yin.shape[1:], F32)

    def carry_on(p):
        @pl.when(jnp.logical_not(starts[p]))
        def _():
            for c in range(chunks):
                hop(p, c).wait_recv()

                @pl.when(jnp.logical_not(gives_all[p]))
                def _():
                    cross(p, c, zin).start()

                own[p, c] = own[p, c] + zin[p, c]

                @pl.when(jnp.logical_not(ends[p]))
                def _():
                    hop(p, c).start()

                @pl.when(gives_all[p])
                def _():
                    cross(p, c, own).start()

    def carried(p, i):
        @pl.when(jnp.logical_not(starts[p] & gives_all[p]))
        def _():
            for j in range(PARTS):
                cross(p, i * PARTS + j, own).wait_recv()

        pieces = [zin[p, i * PARTS + j] + yin[p, i * PARTS + j] for j in range(PARTS)]
        return jnp.concatenate(pieces, axis=0).astype(BF16)

    def drain(p):
        for c in range(chunks):
            @pl.when(jnp.logical_not(ends[p]))
            def _():
                hop(p, c).wait_send()

            @pl.when(gives_all[p] | jnp.logical_not(starts[p]))
            def _():
                cross(p, c, own).wait_send()

    for i in range(heads):
        keep(0, i, dot(k_ref[:, cols(i)], v_ref[:, cols(i)], TN))

    pl.semaphore_wait(barrier, n_head + inner[0].astype(jnp.int32) + inner[1].astype(jnp.int32))
    send_first(0)
    clear(0)
    clear(1)

    along = jnp.broadcast_to(seg_ref[...], (length, length))
    row_ids = lax.broadcasted_iota(jnp.int32, (length, length), 0)
    col_ids = lax.broadcasted_iota(jnp.int32, (length, length), 1)
    allowed = (along.T == along) & (col_ids <= row_ids)
    for i in range(heads):
        raw = dot(q_ref[:, cols(i)], k_ref[:, cols(i)], NT)
        scores[i] = jnp.where(allowed, raw, 0.0).astype(BF16)
        attn[:, cols(i)] = dot(scores[i], v_ref[:, cols(i)], NN)

    carry_on(0)

    squares = jnp.zeros((length, HD), F32)
    products = jnp.zeros((length, HD), F32)
    for i in range(heads):
        state_b[i] = carried(0, i)
        flat = attn[:, cols(i)] + dot(q_ref[:, cols(i)], state_b[i], NN)
        attn[:, cols(i)] = flat
        gained = gain_ref[:, cols(i)] * dy_ref[:, cols(i)].astype(F32)
        squares = squares + flat * flat
        products = products + gained * flat

    norm_out[0:1] = jnp.sum(squares.T, axis=0, keepdims=True)
    norm_out[1:2] = jnp.sum(products.T, axis=0, keepdims=True)
    norm_out[2:8] = jnp.zeros((6, length), F32)

    def share(k):
        return pltpu.make_async_remote_copy(
            src_ref=norm_out, dst_ref=norm_in.at[k - 1], send_sem=ns.at[k - 1],
            recv_sem=nr.at[k - 1], device_id=(s, peer(k)), device_id_type=MESH,
        )

    for k in range(1, n_head):
        share(k).start()
    total = norm_out[...]
    for k in range(1, n_head):
        share(k).wait_recv()
        total = total + norm_in[k - 1]
    inverse_row = lax.rsqrt(total[0:1] / features + 1e-06)
    beta_row = total[1:2] * (inverse_row * inverse_row * inverse_row) / features
    inverse = jnp.broadcast_to(inverse_row, (HD, length)).T
    beta = jnp.broadcast_to(beta_row, (HD, length)).T

    for i in range(heads):
        gained = gain_ref[:, cols(i)] * dy_ref[:, cols(i)].astype(F32)
        dattn[i] = (gained * inverse - attn[:, cols(i)] * beta).astype(BF16)
        keep(1, i, dot(q_ref[:, cols(i)], dattn[i], TN))
    send_first(1)

    for i in range(heads):
        raw = dot(dattn[i], v_ref[:, cols(i)], NT)
        dscores = jnp.where(allowed, raw, 0.0).astype(BF16)
        gq = dot(dscores, k_ref[:, cols(i)], NN) + dot(dattn[i], state_b[i], NT)
        gq_ref[:, cols(i)] = gq.astype(BF16)
        part_k[i] = dot(dscores, q_ref[:, cols(i)], TN)
        part_v[i] = dot(scores[i], dattn[i], TN)
        out = gain_ref[:, cols(i)] * attn[:, cols(i)] * inverse
        out_ref[:, cols(i)] = out.astype(BF16)

    carry_on(1)

    for i in range(heads):
        later_b = carried(1, i)
        gk = part_k[i] + dot(v_ref[:, cols(i)], later_b, NT)
        gk_ref[:, cols(i)] = gk.astype(BF16)
        gv = part_v[i] + dot(k_ref[:, cols(i)], later_b, NN)
        gv_ref[:, cols(i)] = gv.astype(BF16)

    drain(0)
    drain(1)
    for k in range(1, n_head):
        share(k).wait_send()


def on_device(n_seq, n_head, queries, keys, values, grad_out, gain, segment_ids):
    length, width = queries.shape
    heads = width // HD
    chunks = heads * PARTS
    vmem = pl.BlockSpec(memory_space=pltpu.VMEM)
    states = pltpu.VMEM((2, chunks, HD // PARTS, HD), F32)
    return pl.pallas_call(
        functools.partial(kernel, n_seq, n_head, heads),
        out_shape=[jax.ShapeDtypeStruct((length, width), BF16)] * 4,
        in_specs=[vmem] * 6,
        out_specs=[vmem] * 4,
        scratch_shapes=[
            states,
            states,
            states,
            pltpu.VMEM((heads, length, length), BF16),
            pltpu.VMEM((heads, HD, HD), BF16),
            pltpu.VMEM((length, width), F32),
            pltpu.VMEM((heads, length, HD), BF16),
            pltpu.VMEM((heads, length, HD), F32),
            pltpu.VMEM((heads, length, HD), F32),
            pltpu.VMEM((8, length), F32),
            pltpu.VMEM((n_head - 1, 8, length), F32),
            pltpu.SemaphoreType.DMA((2, chunks)),
            pltpu.SemaphoreType.DMA((2, chunks)),
            pltpu.SemaphoreType.DMA((2, chunks)),
            pltpu.SemaphoreType.DMA((2, chunks)),
            pltpu.SemaphoreType.DMA((n_head - 1,)),
            pltpu.SemaphoreType.DMA((n_head - 1,)),
        ],
        compiler_params=pltpu.CompilerParams(
            collective_id=0, has_side_effects=True, vmem_limit_bytes=32 * 1024 * 1024
        ),
    )(queries, keys, values, grad_out, gain.reshape(1, width), segment_ids)


def solution(mesh):
    sizes = dict(mesh.shape)
    placed = P("seq", "head")
    return jax.shard_map(
        functools.partial(on_device, sizes["seq"], sizes["head"]),
        mesh=mesh,
        in_specs=(placed, placed, placed, placed, P("head"), P("seq", None)),
        out_specs=(placed,) * 4,
        check_vma=False,
    )
```

```python
import functools

import jax
import jax.numpy as jnp
from jax import lax
from jax.experimental import pallas as pl
from jax.experimental.pallas import tpu as pltpu
from jax.sharding import PartitionSpec as P

HD = 128
INNER = 2
PARTS = 2
VMEM = 65000 * 1024
MESH = pl.DeviceIdType.MESH
F32 = jnp.float32
BF16 = jnp.bfloat16


def dot(a, b, dims):
    return lax.dot_general(a, b, (dims, ((), ())), preferred_element_type=F32)


NN = ((1,), (0,))
NT = ((1,), (1,))
TN = ((0,), (0,))


def kernel(
    n_seq, n_head, heads, direct, rows, q_hbm, k_hbm, v_hbm, dy_hbm, gain_hbm, seg_hbm,
    out_ref, gq_ref, gk_ref, gv_ref,
    q_ref, k_ref, v_ref, dy_ref, gain_ref, seg_ref,
    own, zin, yin, pre, scores, state_b, attn, gained, q_t, dattn, part_k, part_v,
    norm_out, norm_in, loads, zs, zr, ys, yr, ns, nr,
):
    length = q_ref.shape[0]
    features = n_head * heads * HD
    parts = HD // rows
    chunks = heads * parts
    s, h = lax.axis_index("seq"), lax.axis_index("head")
    y, z = lax.rem(s, INNER), s // INNER
    depth = n_seq // INNER
    across = s + 1 - 2 * y
    bottom, top = z == 0, z == depth - 1
    inner = jnp.logical_not(bottom), jnp.logical_not(top)

    def cols(i):
        return slice(i * HD, (i + 1) * HD)

    def peer(k):
        return lax.rem(h + k, n_head)

    def seq_peer(k):
        return lax.rem(s + k, n_seq)

    turns = sorted(range(1, n_seq), key=lambda k: abs(2 * k - n_seq))

    fetches = [
        pltpu.make_async_copy(src, dst, loads.at[i])
        for i, (src, dst) in enumerate((
            (k_hbm, k_ref), (v_hbm, v_ref), (q_hbm, q_ref), (dy_hbm, dy_ref),
            (gain_hbm, gain_ref), (seg_hbm, seg_ref),
        ))
    ]
    for fetch in fetches:
        fetch.start()

    barrier = pltpu.get_barrier_semaphore()

    def greet(device):
        pl.semaphore_signal(barrier, inc=1, device_id=device, device_id_type=MESH)

    for k in range(1, n_head):
        greet((s, peer(k)))
    if direct:
        for k in turns:
            greet((seq_peer(k), h))
        greetings = n_head - 1 + n_seq - 1
    else:
        greet((across, h))

        @pl.when(inner[0])
        def _():
            greet((s - INNER, h))

        @pl.when(inner[1])
        def _():
            greet((s + INNER, h))

        greetings = n_head + inner[0].astype(jnp.int32) + inner[1].astype(jnp.int32)

    starts = (bottom, top)
    ends = (top, bottom)
    nexts = (s + INNER, s - INNER)
    gives_all = (y == 0, y == 1)

    def hop(p, c):
        return pltpu.make_async_remote_copy(
            src_ref=own.at[p, c], dst_ref=zin.at[p, c], send_sem=zs.at[p, c],
            recv_sem=zr.at[p, c], device_id=(nexts[p], h), device_id_type=MESH,
        )

    def cross(p, c, src):
        return pltpu.make_async_remote_copy(
            src_ref=src.at[p, c], dst_ref=yin.at[p, c], send_sem=ys.at[p, c],
            recv_sem=yr.at[p, c], device_id=(across, h), device_id_type=MESH,
        )

    def keep(p, i, term):
        for j in range(parts):
            own[p, i * parts + j] = term[j * rows:(j + 1) * rows]

    def send_first(p):
        @pl.when(starts[p])
        def _():
            for c in range(chunks):
                hop(p, c).start()

                @pl.when(gives_all[p])
                def _():
                    cross(p, c, own).start()

    def clear(p):
        @pl.when(starts[p])
        def _():
            zin[p] = jnp.zeros(zin.shape[1:], F32)

            @pl.when(gives_all[p])
            def _():
                yin[p] = jnp.zeros(yin.shape[1:], F32)

    def carry_on(p):
        @pl.when(jnp.logical_not(starts[p]))
        def _():
            for c in range(chunks):
                hop(p, c).wait_recv()

                @pl.when(jnp.logical_not(gives_all[p]))
                def _():
                    cross(p, c, zin).start()

                own[p, c] = own[p, c] + zin[p, c]

                @pl.when(jnp.logical_not(ends[p]))
                def _():
                    hop(p, c).start()

                @pl.when(gives_all[p])
                def _():
                    cross(p, c, own).start()

    def carried(p, i):
        if direct:
            pieces = [yin[p, i * parts + j] for j in range(parts)]
            return jnp.concatenate(pieces, axis=0).astype(BF16)

        @pl.when(jnp.logical_not(starts[p] & gives_all[p]))
        def _():
            for j in range(parts):
                cross(p, i * parts + j, own).wait_recv()

        pieces = [zin[p, i * parts + j] + yin[p, i * parts + j] for j in range(parts)]
        return jnp.concatenate(pieces, axis=0).astype(BF16)

    def drain(p):
        for c in range(chunks):
            @pl.when(jnp.logical_not(ends[p]))
            def _():
                hop(p, c).wait_send()

            @pl.when(gives_all[p] | jnp.logical_not(starts[p]))
            def _():
                cross(p, c, own).wait_send()

    def scatter(p, k, slot):
        return pltpu.make_async_remote_copy(
            src_ref=own.at[p, seq_peer(k)], dst_ref=zin.at[p, slot], send_sem=zs.at[p, k],
            recv_sem=zr.at[p, slot], device_id=(seq_peer(k), h), device_id_type=MESH,
        )

    def give_back(p, k, slot):
        return pltpu.make_async_remote_copy(
            src_ref=pre.at[p, seq_peer(k)], dst_ref=yin.at[p, slot], send_sem=ys.at[p, k],
            recv_sem=yr.at[p, slot], device_id=(seq_peer(k), h), device_id_type=MESH,
        )

    def begin(p):
        if not direct:
            send_first(p)
            clear(p)
            return
        for k in turns:
            scatter(p, k, s).start()
        zin[p, s] = own[p, s]

    def finish(p):
        if not direct:
            carry_on(p)
            return
        for k in turns:
            scatter(p, k, seq_peer(k)).wait_recv()
        total = jnp.zeros((rows, HD), F32)
        for t in range(n_seq) if p == 0 else reversed(range(n_seq)):
            pre[p, t] = total
            total = total + zin[p, t]
        for k in turns:
            give_back(p, k, s).start()
        yin[p, s] = pre[p, s]
        for k in turns:
            give_back(p, k, seq_peer(k)).wait_recv()

    def settle(p):
        if not direct:
            drain(p)
            return
        for k in turns:
            scatter(p, k, s).wait_send()
            give_back(p, k, s).wait_send()

    fetches[0].wait()
    fetches[1].wait()
    for i in range(heads):
        keep(0, i, dot(k_ref[:, cols(i)], v_ref[:, cols(i)], TN))

    pl.semaphore_wait(barrier, greetings)
    begin(0)
    for fetch in fetches[2:]:
        fetch.wait()

    along = jnp.broadcast_to(seg_ref[...], (length, length))
    row_ids = lax.broadcasted_iota(jnp.int32, (length, length), 0)
    col_ids = lax.broadcasted_iota(jnp.int32, (length, length), 1)
    allowed = (along.T == along) & (col_ids <= row_ids)
    for i in range(heads):
        raw = dot(q_ref[:, cols(i)], k_ref[:, cols(i)], NT)
        scores[i] = jnp.where(allowed, raw, 0.0).astype(BF16)
        attn[:, cols(i)] = dot(scores[i], v_ref[:, cols(i)], NN)
        gained[:, cols(i)] = gain_ref[:, cols(i)] * dy_ref[:, cols(i)].astype(F32)
        q_t[i] = q_ref[:, cols(i)].T

    finish(0)

    squares = jnp.zeros((length, HD), F32)
    products = jnp.zeros((length, HD), F32)
    for i in range(heads):
        state_b[i] = carried(0, i)
        flat = attn[:, cols(i)] + dot(q_ref[:, cols(i)], state_b[i], NN)
        attn[:, cols(i)] = flat
        squares = squares + flat * flat
        products = products + gained[:, cols(i)] * flat

    norm_out[0:1] = jnp.sum(squares.T, axis=0, keepdims=True)
    norm_out[1:2] = jnp.sum(products.T, axis=0, keepdims=True)
    norm_out[2:8] = jnp.zeros((6, length), F32)

    def share(k):
        return pltpu.make_async_remote_copy(
            src_ref=norm_out, dst_ref=norm_in.at[k - 1], send_sem=ns.at[k - 1],
            recv_sem=nr.at[k - 1], device_id=(s, peer(k)), device_id_type=MESH,
        )

    for k in range(1, n_head):
        share(k).start()
    total = norm_out[...]
    for k in range(1, n_head):
        share(k).wait_recv()
        total = total + norm_in[k - 1]
    inverse_row = lax.rsqrt(total[0:1] / features + 1e-06)
    beta_row = total[1:2] * (inverse_row * inverse_row * inverse_row) / features
    inverse = jnp.broadcast_to(inverse_row, (HD, length)).T
    beta = jnp.broadcast_to(beta_row, (HD, length)).T

    for i in range(heads):
        dattn[i] = (gained[:, cols(i)] * inverse - attn[:, cols(i)] * beta).astype(BF16)
        keep(1, i, dot(q_t[i], dattn[i], NN))
    begin(1)

    for i in range(heads):
        raw = dot(dattn[i], v_ref[:, cols(i)], NT)
        dscores = jnp.where(allowed, raw, 0.0).astype(BF16)
        gq = dot(dscores, k_ref[:, cols(i)], NN) + dot(dattn[i], state_b[i], NT)
        gq_ref[:, cols(i)] = gq.astype(BF16)
        part_k[i] = dot(dscores, q_ref[:, cols(i)], TN)
        part_v[i] = dot(scores[i], dattn[i], TN)
        out = gain_ref[:, cols(i)] * attn[:, cols(i)] * inverse
        out_ref[:, cols(i)] = out.astype(BF16)

    finish(1)

    for i in range(heads):
        later_b = carried(1, i)
        gk = part_k[i] + dot(v_ref[:, cols(i)], later_b, NT)
        gk_ref[:, cols(i)] = gk.astype(BF16)
        gv = part_v[i] + dot(k_ref[:, cols(i)], later_b, NN)
        gv_ref[:, cols(i)] = gv.astype(BF16)

    settle(0)
    settle(1)
    for k in range(1, n_head):
        share(k).wait_send()


def write_out(*refs):
    count = len(refs) // 2
    copies = [
        pltpu.make_async_copy(refs[i], refs[count + i], refs[-1].at[i]) for i in range(count)
    ]
    for copy in copies:
        copy.start()
    for copy in copies:
        copy.wait()


def on_device(n_seq, n_head, queries, keys, values, grad_out, gain, segment_ids):
    length, width = queries.shape
    heads = width // HD
    rows = width // n_seq
    direct = width % n_seq == 0 and rows % 8 == 0 and HD % rows == 0
    if not direct:
        rows = HD // PARTS
    chunks = width // rows
    vmem = pl.BlockSpec(memory_space=pltpu.VMEM)
    hbm = pl.BlockSpec(memory_space=pl.ANY)
    states = pltpu.VMEM((2, chunks, rows, HD), F32)
    tokens = pltpu.VMEM((length, width), BF16)
    wide = pltpu.VMEM((length, width), F32)
    per_head = pltpu.VMEM((heads, length, HD), F32)
    flags = pltpu.SemaphoreType.DMA((2, chunks))
    results = pl.pallas_call(
        functools.partial(kernel, n_seq, n_head, heads, direct, rows),
        out_shape=[jax.ShapeDtypeStruct((length, width), BF16)] * 4,
        in_specs=[hbm] * 6,
        out_specs=[vmem] * 4,
        scratch_shapes=[
            tokens,
            tokens,
            tokens,
            tokens,
            pltpu.VMEM((1, width), F32),
            pltpu.VMEM((1, length), jnp.int32),
            states,
            states,
            states,
            states,
            pltpu.VMEM((heads, length, length), BF16),
            pltpu.VMEM((heads, HD, HD), BF16),
            wide,
            wide,
            pltpu.VMEM((heads, HD, length), BF16),
            pltpu.VMEM((heads, length, HD), BF16),
            per_head,
            per_head,
            pltpu.VMEM((8, length), F32),
            pltpu.VMEM((n_head - 1, 8, length), F32),
            pltpu.SemaphoreType.DMA((6,)),
            flags,
            flags,
            flags,
            flags,
            pltpu.SemaphoreType.DMA((n_head - 1,)),
            pltpu.SemaphoreType.DMA((n_head - 1,)),
        ],
        compiler_params=pltpu.CompilerParams(
            collective_id=0, has_side_effects=True, vmem_limit_bytes=VMEM
        ),
    )(queries, keys, values, grad_out, gain.reshape(1, width), segment_ids)
    return pl.pallas_call(
        write_out,
        out_shape=[jax.ShapeDtypeStruct((length, width), BF16)] * 4,
        in_specs=[hbm] * 4,
        out_specs=[hbm] * 4,
        scratch_shapes=[pltpu.SemaphoreType.DMA((4,))],
        compiler_params=pltpu.CompilerParams(vmem_limit_bytes=VMEM),
    )(*results)


def solution(mesh):
    sizes = dict(mesh.shape)
    placed = P("seq", "head")
    return jax.shard_map(
        functools.partial(on_device, sizes["seq"], sizes["head"]),
        mesh=mesh,
        in_specs=(placed, placed, placed, placed, P("head"), P("seq", None)),
        out_specs=(placed,) * 4,
        check_vma=False,
    )
```

```python
import functools

import jax
import jax.numpy as jnp
from jax import lax
from jax.experimental import pallas as pl
from jax.experimental.pallas import tpu as pltpu
from jax.sharding import PartitionSpec as P

HD = 128
INNER = 2
PARTS = 4
VMEM = 65000 * 1024
MESH = pl.DeviceIdType.MESH
F32 = jnp.float32
BF16 = jnp.bfloat16


def dot(a, b, dims):
    return lax.dot_general(a, b, (dims, ((), ())), preferred_element_type=F32)


NN = ((1,), (0,))
NT = ((1,), (1,))
TN = ((0,), (0,))


def kernel(
    n_seq, n_head, heads, q_hbm, k_hbm, v_hbm, dy_hbm, gain_hbm, seg_hbm,
    out_hbm, gq_hbm, gk_hbm, gv_hbm,
    out_ref, gq_ref, gk_ref, gv_ref,
    q_ref, k_ref, v_ref, dy_ref, gain_ref, seg_ref,
    own, zin, yin, scores, state_b, attn, gained, q_t, dattn, part_k, part_v,
    norm_out, norm_in, loads, stores, zs, zr, ys, yr, ns, nr,
):
    length = q_ref.shape[0]
    features = n_head * heads * HD
    rows = HD // PARTS
    chunks = heads * PARTS
    s, h = lax.axis_index("seq"), lax.axis_index("head")
    y, z = lax.rem(s, INNER), s // INNER
    depth = n_seq // INNER
    across = s + 1 - 2 * y
    bottom, top = z == 0, z == depth - 1
    inner = jnp.logical_not(bottom), jnp.logical_not(top)

    def cols(i):
        return slice(i * HD, (i + 1) * HD)

    def peer(k):
        return lax.rem(h + k, n_head)

    fetches = [
        pltpu.make_async_copy(src, dst, loads.at[i])
        for i, (src, dst) in enumerate((
            (k_hbm, k_ref), (v_hbm, v_ref), (q_hbm, q_ref), (dy_hbm, dy_ref),
            (gain_hbm, gain_ref), (seg_hbm, seg_ref),
        ))
    ]
    for fetch in fetches:
        fetch.start()
    writes = [
        pltpu.make_async_copy(src, dst, stores.at[i])
        for i, (src, dst) in enumerate((
            (out_ref, out_hbm), (gq_ref, gq_hbm), (gk_ref, gk_hbm), (gv_ref, gv_hbm),
        ))
    ]

    barrier = pltpu.get_barrier_semaphore()

    def greet(device):
        pl.semaphore_signal(barrier, inc=1, device_id=device, device_id_type=MESH)

    for k in range(1, n_head):
        greet((s, peer(k)))
    greet((across, h))

    @pl.when(inner[0])
    def _():
        greet((s - INNER, h))

    @pl.when(inner[1])
    def _():
        greet((s + INNER, h))

    greetings = n_head + inner[0].astype(jnp.int32) + inner[1].astype(jnp.int32)

    starts = (bottom, top)
    ends = (top, bottom)
    nexts = (s + INNER, s - INNER)
    gives_all = (y == 0, y == 1)

    def hop(p, c):
        return pltpu.make_async_remote_copy(
            src_ref=own.at[p, c], dst_ref=zin.at[p, c], send_sem=zs.at[p, c],
            recv_sem=zr.at[p, c], device_id=(nexts[p], h), device_id_type=MESH,
        )

    def cross(p, c, src):
        return pltpu.make_async_remote_copy(
            src_ref=src.at[p, c], dst_ref=yin.at[p, c], send_sem=ys.at[p, c],
            recv_sem=yr.at[p, c], device_id=(across, h), device_id_type=MESH,
        )

    def keep(p, i, term):
        for j in range(PARTS):
            own[p, i * PARTS + j] = term[j * rows:(j + 1) * rows]

    def send_first(p, chunk_ids):
        @pl.when(starts[p])
        def _():
            for c in chunk_ids:
                hop(p, c).start()

                @pl.when(gives_all[p])
                def _():
                    cross(p, c, own).start()

    def clear(p):
        @pl.when(starts[p])
        def _():
            zin[p] = jnp.zeros(zin.shape[1:], F32)

            @pl.when(gives_all[p])
            def _():
                yin[p] = jnp.zeros(yin.shape[1:], F32)

    def carry_on(p):
        @pl.when(jnp.logical_not(starts[p]))
        def _():
            for c in range(chunks):
                hop(p, c).wait_recv()

                own[p, c] = own[p, c] + zin[p, c]

                @pl.when(jnp.logical_not(ends[p]))
                def _():
                    hop(p, c).start()

                @pl.when(gives_all[p])
                def _():
                    cross(p, c, own).start()

                @pl.when(jnp.logical_not(gives_all[p]))
                def _():
                    cross(p, c, zin).start()

    def carried(p, i):
        @pl.when(jnp.logical_not(starts[p] & gives_all[p]))
        def _():
            for j in range(PARTS):
                cross(p, i * PARTS + j, own).wait_recv()

        pieces = [zin[p, i * PARTS + j] + yin[p, i * PARTS + j] for j in range(PARTS)]
        return jnp.concatenate(pieces, axis=0).astype(BF16)

    def drain(p):
        for c in range(chunks):
            @pl.when(jnp.logical_not(ends[p]))
            def _():
                hop(p, c).wait_send()

            @pl.when(gives_all[p] | jnp.logical_not(starts[p]))
            def _():
                cross(p, c, own).wait_send()

    fetches[0].wait()
    fetches[1].wait()
    for i in range(heads):
        keep(0, i, dot(k_ref[:, cols(i)], v_ref[:, cols(i)], TN))

    pl.semaphore_wait(barrier, greetings)
    send_first(0, range(chunks))
    clear(0)
    clear(1)
    for fetch in fetches[2:]:
        fetch.wait()

    along = jnp.broadcast_to(seg_ref[...], (length, length))
    row_ids = lax.broadcasted_iota(jnp.int32, (length, length), 0)
    col_ids = lax.broadcasted_iota(jnp.int32, (length, length), 1)
    allowed = (along.T == along) & (col_ids <= row_ids)
    for i in range(heads):
        raw = dot(q_ref[:, cols(i)], k_ref[:, cols(i)], NT)
        scores[i] = jnp.where(allowed, raw, 0.0).astype(BF16)
        attn[:, cols(i)] = dot(scores[i], v_ref[:, cols(i)], NN)
        gained[:, cols(i)] = gain_ref[:, cols(i)] * dy_ref[:, cols(i)].astype(F32)
        q_t[i] = q_ref[:, cols(i)].T

    carry_on(0)

    squares = jnp.zeros((length, HD), F32)
    products = jnp.zeros((length, HD), F32)
    for i in range(heads):
        state_b[i] = carried(0, i)
        flat = attn[:, cols(i)] + dot(q_ref[:, cols(i)], state_b[i], NN)
        attn[:, cols(i)] = flat
        squares = squares + flat * flat
        products = products + gained[:, cols(i)] * flat

    norm_out[0:1] = jnp.sum(squares.T, axis=0, keepdims=True)
    norm_out[1:2] = jnp.sum(products.T, axis=0, keepdims=True)
    norm_out[2:8] = jnp.zeros((6, length), F32)

    def share(k):
        return pltpu.make_async_remote_copy(
            src_ref=norm_out, dst_ref=norm_in.at[k - 1], send_sem=ns.at[k - 1],
            recv_sem=nr.at[k - 1], device_id=(s, peer(k)), device_id_type=MESH,
        )

    for k in range(1, n_head):
        share(k).start()
    total = norm_out[...]
    for k in range(1, n_head):
        share(k).wait_recv()
        total = total + norm_in[k - 1]
    inverse_row = lax.rsqrt(total[0:1] / features + 1e-06)
    beta_row = total[1:2] * (inverse_row * inverse_row * inverse_row) / features
    inverse = jnp.broadcast_to(inverse_row, (HD, length)).T
    beta = jnp.broadcast_to(beta_row, (HD, length)).T

    for i in range(heads):
        dattn[i] = (gained[:, cols(i)] * inverse - attn[:, cols(i)] * beta).astype(BF16)
        keep(1, i, dot(q_t[i], dattn[i], NN))
        send_first(1, range(i * PARTS, (i + 1) * PARTS))

    for i in range(heads):
        raw = dot(dattn[i], v_ref[:, cols(i)], NT)
        dscores = jnp.where(allowed, raw, 0.0).astype(BF16)
        gq = dot(dscores, k_ref[:, cols(i)], NN) + dot(dattn[i], state_b[i], NT)
        gq_ref[:, cols(i)] = gq.astype(BF16)
        part_k[i] = dot(dscores, q_ref[:, cols(i)], TN)
        part_v[i] = dot(scores[i], dattn[i], TN)
        out = gain_ref[:, cols(i)] * attn[:, cols(i)] * inverse
        out_ref[:, cols(i)] = out.astype(BF16)

    writes[0].start()
    writes[1].start()

    carry_on(1)

    for i in range(heads):
        later_b = carried(1, i)
        gk = part_k[i] + dot(v_ref[:, cols(i)], later_b, NT)
        gk_ref[:, cols(i)] = gk.astype(BF16)
        gv = part_v[i] + dot(k_ref[:, cols(i)], later_b, NN)
        gv_ref[:, cols(i)] = gv.astype(BF16)

    writes[2].start()
    writes[3].start()
    drain(0)
    drain(1)
    for k in range(1, n_head):
        share(k).wait_send()
    for write in writes:
        write.wait()


def write_out(*refs):
    sources, targets, held, come, go = refs[:4], refs[4:8], refs[8:12], refs[12], refs[13]
    reads = [pltpu.make_async_copy(a, b, come.at[i]) for i, (a, b) in enumerate(zip(sources, held))]
    writes = [pltpu.make_async_copy(a, b, go.at[i]) for i, (a, b) in enumerate(zip(held, targets))]
    for read in reads:
        read.start()
    for read, write in zip(reads, writes):
        read.wait()
        write.start()
    for write in writes:
        write.wait()


def on_device(n_seq, n_head, queries, keys, values, grad_out, gain, segment_ids):
    length, width = queries.shape
    heads = width // HD
    chunks = heads * PARTS
    hbm = pl.BlockSpec(memory_space=pl.ANY)
    states = pltpu.VMEM((2, chunks, HD // PARTS, HD), F32)
    tokens = pltpu.VMEM((length, width), BF16)
    wide = pltpu.VMEM((length, width), F32)
    per_head = pltpu.VMEM((heads, length, HD), F32)
    flags = pltpu.SemaphoreType.DMA((2, chunks))
    results = pl.pallas_call(
        functools.partial(kernel, n_seq, n_head, heads),
        out_shape=[jax.ShapeDtypeStruct((length, width), BF16)] * 4,
        in_specs=[hbm] * 6,
        out_specs=[hbm] * 4,
        scratch_shapes=[tokens] * 4 + [
            tokens,
            tokens,
            tokens,
            tokens,
            pltpu.VMEM((1, width), F32),
            pltpu.VMEM((1, length), jnp.int32),
            states,
            states,
            states,
            pltpu.VMEM((heads, length, length), BF16),
            pltpu.VMEM((heads, HD, HD), BF16),
            wide,
            wide,
            pltpu.VMEM((heads, HD, length), BF16),
            pltpu.VMEM((heads, length, HD), BF16),
            per_head,
            per_head,
            pltpu.VMEM((8, length), F32),
            pltpu.VMEM((n_head - 1, 8, length), F32),
            pltpu.SemaphoreType.DMA((6,)),
            pltpu.SemaphoreType.DMA((4,)),
            flags,
            flags,
            flags,
            flags,
            pltpu.SemaphoreType.DMA((n_head - 1,)),
            pltpu.SemaphoreType.DMA((n_head - 1,)),
        ],
        compiler_params=pltpu.CompilerParams(
            collective_id=0, has_side_effects=True, vmem_limit_bytes=VMEM,
        ),
    )(queries, keys, values, grad_out, gain.reshape(1, width), segment_ids)
    return pl.pallas_call(
        write_out,
        out_shape=[jax.ShapeDtypeStruct((length, width), BF16)] * 4,
        in_specs=[hbm] * 4,
        out_specs=[hbm] * 4,
        scratch_shapes=[tokens] * 4 + [pltpu.SemaphoreType.DMA((4,))] * 2,
        compiler_params=pltpu.CompilerParams(vmem_limit_bytes=VMEM),
    )(*results)


def solution(mesh):
    sizes = dict(mesh.shape)
    placed = P("seq", "head")
    return jax.shard_map(
        functools.partial(on_device, sizes["seq"], sizes["head"]),
        mesh=mesh,
        in_specs=(placed, placed, placed, placed, P("head"), P("seq", None)),
        out_specs=(placed,) * 4,
        check_vma=False,
    )
```

```python
import functools

import jax
import jax.numpy as jnp
from jax import lax
from jax.experimental import pallas as pl
from jax.experimental.pallas import tpu as pltpu
from jax.sharding import PartitionSpec as P

HD = 128
INNER = 2
PARTS = 4
VMEM = 65000 * 1024
MESH = pl.DeviceIdType.MESH
F32 = jnp.float32
BF16 = jnp.bfloat16


def dot(a, b, dims):
    return lax.dot_general(a, b, (dims, ((), ())), preferred_element_type=F32)


NN = ((1,), (0,))
NT = ((1,), (1,))
TN = ((0,), (0,))


def kernel(
    n_seq, n_head, heads, q_hbm, k_hbm, v_hbm, dy_hbm, gain_hbm, seg_hbm,
    out_hbm, gq_hbm, gk_hbm, gv_hbm,
    out_ref, gq_ref, gk_ref, gv_ref,
    q_ref, k_ref, v_ref, dy_ref, gain_ref, seg_ref,
    own, tot, zin, yin, raw_in, scores, state_b, attn, gained, q_t, dattn, part_k, part_v,
    norm_out, norm_in, loads, stores, zs, zr, ys, yr, rs, rr, ns, nr,
):
    length = q_ref.shape[0]
    features = n_head * heads * HD
    rows = HD // PARTS
    chunks = heads * PARTS
    s, h = lax.axis_index("seq"), lax.axis_index("head")
    y, z = lax.rem(s, INNER), s // INNER
    depth = n_seq // INNER
    across = s + 1 - 2 * y
    bottom, top = z == 0, z == depth - 1
    inner = jnp.logical_not(bottom), jnp.logical_not(top)

    def cols(i):
        return slice(i * HD, (i + 1) * HD)

    def peer(k):
        return lax.rem(h + k, n_head)

    fetches = [
        pltpu.make_async_copy(src, dst, loads.at[i])
        for i, (src, dst) in enumerate((
            (k_hbm, k_ref), (v_hbm, v_ref), (q_hbm, q_ref), (dy_hbm, dy_ref),
            (gain_hbm, gain_ref), (seg_hbm, seg_ref),
        ))
    ]
    for fetch in fetches:
        fetch.start()
    writes = [
        pltpu.make_async_copy(src, dst, stores.at[i])
        for i, (src, dst) in enumerate((
            (out_ref, out_hbm), (gq_ref, gq_hbm), (gk_ref, gk_hbm), (gv_ref, gv_hbm),
        ))
    ]

    barrier = pltpu.get_barrier_semaphore()

    def greet(device):
        pl.semaphore_signal(barrier, inc=1, device_id=device, device_id_type=MESH)

    for k in range(1, n_head):
        greet((s, peer(k)))
    greet((across, h))

    @pl.when(inner[0])
    def _():
        greet((s - INNER, h))
        greet((across - INNER, h))

    @pl.when(inner[1])
    def _():
        greet((s + INNER, h))
        greet((across + INNER, h))

    greetings = n_head + 2 * inner[0].astype(jnp.int32) + 2 * inner[1].astype(jnp.int32)

    starts = (bottom, top)
    ends = (top, bottom)
    seconds = (z == 1, z == depth - 2)
    steps = (INNER, -INNER)
    takes_pair = (y == 1, y == 0)

    def hop(p, c, src):
        return pltpu.make_async_remote_copy(
            src_ref=src.at[p, c], dst_ref=zin.at[p, c], send_sem=zs.at[p, c],
            recv_sem=zr.at[p, c], device_id=(s + steps[p], h), device_id_type=MESH,
        )

    def slant(p, c):
        return pltpu.make_async_remote_copy(
            src_ref=own.at[p, c], dst_ref=raw_in.at[p, c], send_sem=rs.at[p, c],
            recv_sem=rr.at[p, c], device_id=(across + steps[p], h), device_id_type=MESH,
        )

    def cross(p, c):
        return pltpu.make_async_remote_copy(
            src_ref=own.at[p, c], dst_ref=yin.at[p, c], send_sem=ys.at[p, c],
            recv_sem=yr.at[p, c], device_id=(across, h), device_id_type=MESH,
        )

    def keep(p, i, term):
        for j in range(PARTS):
            own[p, i * PARTS + j] = term[j * rows:(j + 1) * rows]

    def send_own(p, chunk_ids):
        for c in chunk_ids:
            cross(p, c).start()
            if c < PARTS:
                @pl.when(starts[p])
                def _():
                    hop(p, c, own).start()
                    slant(p, c).start()

    def carry_on(p):
        @pl.when(starts[p])
        def _():
            zin[p] = jnp.zeros(zin.shape[1:], F32)
            for c in range(PARTS, chunks):
                cross(p, c).wait_recv()
                tot[p, c] = own[p, c] + yin[p, c]
                hop(p, c, tot).start()
            for c in range(PARTS):
                cross(p, c).wait_recv()

        @pl.when(jnp.logical_not(starts[p]))
        def _():
            for c in range(chunks):
                cross(p, c).wait_recv()
                hop(p, c, tot).wait_recv()
                if c < PARTS:
                    @pl.when(seconds[p])
                    def _():
                        slant(p, c).wait_recv()
                        zin[p, c] = zin[p, c] + raw_in[p, c]

                @pl.when(jnp.logical_not(ends[p]))
                def _():
                    tot[p, c] = own[p, c] + yin[p, c] + zin[p, c]
                    hop(p, c, tot).start()

    def carried(p, i):
        pieces = [
            zin[p, c] + jnp.where(takes_pair[p], yin[p, c], 0.0)
            for c in range(i * PARTS, (i + 1) * PARTS)
        ]
        return jnp.concatenate(pieces, axis=0).astype(BF16)

    def drain(p):
        for c in range(chunks):
            cross(p, c).wait_send()

        @pl.when(jnp.logical_not(ends[p]))
        def _():
            for c in range(chunks):
                hop(p, c, tot).wait_send()

        @pl.when(starts[p])
        def _():
            for c in range(PARTS):
                slant(p, c).wait_send()

    fetches[0].wait()
    fetches[1].wait()
    for i in range(heads):
        keep(0, i, dot(k_ref[:, cols(i)], v_ref[:, cols(i)], TN))

    pl.semaphore_wait(barrier, greetings)
    send_own(0, range(chunks))
    for fetch in fetches[2:]:
        fetch.wait()

    along = jnp.broadcast_to(seg_ref[...], (length, length))
    row_ids = lax.broadcasted_iota(jnp.int32, (length, length), 0)
    col_ids = lax.broadcasted_iota(jnp.int32, (length, length), 1)
    allowed = (along.T == along) & (col_ids <= row_ids)
    for i in range(heads):
        raw = dot(q_ref[:, cols(i)], k_ref[:, cols(i)], NT)
        scores[i] = jnp.where(allowed, raw, 0.0).astype(BF16)
        attn[:, cols(i)] = dot(scores[i], v_ref[:, cols(i)], NN)
        gained[:, cols(i)] = gain_ref[:, cols(i)] * dy_ref[:, cols(i)].astype(F32)
        q_t[i] = q_ref[:, cols(i)].T

    carry_on(0)

    squares = jnp.zeros((length, HD), F32)
    products = jnp.zeros((length, HD), F32)
    for i in range(heads):
        state_b[i] = carried(0, i)
        flat = attn[:, cols(i)] + dot(q_ref[:, cols(i)], state_b[i], NN)
        attn[:, cols(i)] = flat
        squares = squares + flat * flat
        products = products + gained[:, cols(i)] * flat

    norm_out[0:1] = jnp.sum(squares.T, axis=0, keepdims=True)
    norm_out[1:2] = jnp.sum(products.T, axis=0, keepdims=True)
    norm_out[2:8] = jnp.zeros((6, length), F32)

    def share(k):
        return pltpu.make_async_remote_copy(
            src_ref=norm_out, dst_ref=norm_in.at[k - 1], send_sem=ns.at[k - 1],
            recv_sem=nr.at[k - 1], device_id=(s, peer(k)), device_id_type=MESH,
        )

    for k in range(1, n_head):
        share(k).start()
    total = norm_out[...]
    for k in range(1, n_head):
        share(k).wait_recv()
        total = total + norm_in[k - 1]
    inverse_row = lax.rsqrt(total[0:1] / features + 1e-06)
    beta_row = total[1:2] * (inverse_row * inverse_row * inverse_row) / features
    inverse = jnp.broadcast_to(inverse_row, (HD, length)).T
    beta = jnp.broadcast_to(beta_row, (HD, length)).T

    for i in range(heads):
        dattn[i] = (gained[:, cols(i)] * inverse - attn[:, cols(i)] * beta).astype(BF16)
        keep(1, i, dot(q_t[i], dattn[i], NN))
        send_own(1, range(i * PARTS, (i + 1) * PARTS))

    for i in range(heads):
        raw = dot(dattn[i], v_ref[:, cols(i)], NT)
        dscores = jnp.where(allowed, raw, 0.0).astype(BF16)
        gq = dot(dscores, k_ref[:, cols(i)], NN) + dot(dattn[i], state_b[i], NT)
        gq_ref[:, cols(i)] = gq.astype(BF16)
        part_k[i] = dot(dscores, q_ref[:, cols(i)], TN)
        part_v[i] = dot(scores[i], dattn[i], TN)
        out = gain_ref[:, cols(i)] * attn[:, cols(i)] * inverse
        out_ref[:, cols(i)] = out.astype(BF16)

    writes[0].start()
    writes[1].start()

    carry_on(1)

    for i in range(heads):
        later_b = carried(1, i)
        gk = part_k[i] + dot(v_ref[:, cols(i)], later_b, NT)
        gk_ref[:, cols(i)] = gk.astype(BF16)
        gv = part_v[i] + dot(k_ref[:, cols(i)], later_b, NN)
        gv_ref[:, cols(i)] = gv.astype(BF16)

    writes[2].start()
    writes[3].start()
    drain(0)
    drain(1)
    for k in range(1, n_head):
        share(k).wait_send()
    for write in writes:
        write.wait()


def write_out(*refs):
    sources, targets, held, come, go = refs[:4], refs[4:8], refs[8:12], refs[12], refs[13]
    reads = [pltpu.make_async_copy(a, b, come.at[i]) for i, (a, b) in enumerate(zip(sources, held))]
    writes = [pltpu.make_async_copy(a, b, go.at[i]) for i, (a, b) in enumerate(zip(held, targets))]
    for read in reads:
        read.start()
    for read, write in zip(reads, writes):
        read.wait()
        write.start()
    for write in writes:
        write.wait()


def on_device(n_seq, n_head, queries, keys, values, grad_out, gain, segment_ids):
    length, width = queries.shape
    heads = width // HD
    chunks = heads * PARTS
    hbm = pl.BlockSpec(memory_space=pl.ANY)
    states = pltpu.VMEM((2, chunks, HD // PARTS, HD), F32)
    tokens = pltpu.VMEM((length, width), BF16)
    wide = pltpu.VMEM((length, width), F32)
    per_head = pltpu.VMEM((heads, length, HD), F32)
    flags = pltpu.SemaphoreType.DMA((2, chunks))
    results = pl.pallas_call(
        functools.partial(kernel, n_seq, n_head, heads),
        out_shape=[jax.ShapeDtypeStruct((length, width), BF16)] * 4,
        in_specs=[hbm] * 6,
        out_specs=[hbm] * 4,
        scratch_shapes=[tokens] * 4 + [
            tokens,
            tokens,
            tokens,
            tokens,
            pltpu.VMEM((1, width), F32),
            pltpu.VMEM((1, length), jnp.int32),
            states,
            states,
            states,
            states,
            pltpu.VMEM((2, PARTS, HD // PARTS, HD), F32),
            pltpu.VMEM((heads, length, length), BF16),
            pltpu.VMEM((heads, HD, HD), BF16),
            wide,
            wide,
            pltpu.VMEM((heads, HD, length), BF16),
            pltpu.VMEM((heads, length, HD), BF16),
            per_head,
            per_head,
            pltpu.VMEM((8, length), F32),
            pltpu.VMEM((n_head - 1, 8, length), F32),
            pltpu.SemaphoreType.DMA((6,)),
            pltpu.SemaphoreType.DMA((4,)),
            flags,
            flags,
            flags,
            flags,
            pltpu.SemaphoreType.DMA((2, PARTS)),
            pltpu.SemaphoreType.DMA((2, PARTS)),
            pltpu.SemaphoreType.DMA((n_head - 1,)),
            pltpu.SemaphoreType.DMA((n_head - 1,)),
        ],
        compiler_params=pltpu.CompilerParams(
            collective_id=0, has_side_effects=True, vmem_limit_bytes=VMEM,
        ),
    )(queries, keys, values, grad_out, gain.reshape(1, width), segment_ids)
    return pl.pallas_call(
        write_out,
        out_shape=[jax.ShapeDtypeStruct((length, width), BF16)] * 4,
        in_specs=[hbm] * 4,
        out_specs=[hbm] * 4,
        scratch_shapes=[tokens] * 4 + [pltpu.SemaphoreType.DMA((4,))] * 2,
        compiler_params=pltpu.CompilerParams(vmem_limit_bytes=VMEM),
    )(*results)


def solution(mesh):
    sizes = dict(mesh.shape)
    placed = P("seq", "head")
    return jax.shard_map(
        functools.partial(on_device, sizes["seq"], sizes["head"]),
        mesh=mesh,
        in_specs=(placed, placed, placed, placed, P("head"), P("seq", None)),
        out_specs=(placed,) * 4,
        check_vma=False,
    )
```

```python
import functools

import jax
import jax.numpy as jnp
from jax import lax
from jax.experimental import pallas as pl
from jax.experimental.pallas import tpu as pltpu
from jax.sharding import PartitionSpec as P

HD = 128
INNER = 2
PARTS = 4
VMEM = 65000 * 1024
MESH = pl.DeviceIdType.MESH
F32 = jnp.float32
BF16 = jnp.bfloat16


def dot(a, b, dims):
    return lax.dot_general(a, b, (dims, ((), ())), preferred_element_type=F32)


NN = ((1,), (0,))
NT = ((1,), (1,))
TN = ((0,), (0,))


def kernel(
    n_seq, n_head, heads, q_hbm, k_hbm, v_hbm, dy_hbm, gain_hbm, seg_hbm,
    out_hbm, gq_hbm, gk_hbm, gv_hbm,
    out_ref, gq_ref, gk_ref, gv_ref,
    q_ref, k_ref, v_ref, dy_ref, gain_ref, seg_ref,
    own, tot, zin, yin, slant_in, scores, state_b, attn, gained, q_t, dattn, part_k, part_v,
    norm_out, norm_in, loads, stores, zs, zr, ys, yr, rs, rr, ns, nr,
):
    length = q_ref.shape[0]
    features = n_head * heads * HD
    rows = HD // PARTS
    chunks = heads * PARTS
    plain = chunks - PARTS
    s, h = lax.axis_index("seq"), lax.axis_index("head")
    y, z = lax.rem(s, INNER), s // INNER
    depth = n_seq // INNER
    across = s + 1 - 2 * y
    bottom, top = z == 0, z == depth - 1
    inner = jnp.logical_not(bottom), jnp.logical_not(top)

    def cols(i):
        return slice(i * HD, (i + 1) * HD)

    def peer(k):
        return lax.rem(h + k, n_head)

    fetches = [
        pltpu.make_async_copy(src, dst, loads.at[i])
        for i, (src, dst) in enumerate((
            (k_hbm, k_ref), (v_hbm, v_ref), (q_hbm, q_ref), (dy_hbm, dy_ref),
            (gain_hbm, gain_ref), (seg_hbm, seg_ref),
        ))
    ]
    for fetch in fetches:
        fetch.start()
    writes = [
        pltpu.make_async_copy(src, dst, stores.at[i])
        for i, (src, dst) in enumerate((
            (out_ref, out_hbm), (gq_ref, gq_hbm), (gk_ref, gk_hbm), (gv_ref, gv_hbm),
        ))
    ]

    barrier = pltpu.get_barrier_semaphore()

    def greet(device):
        pl.semaphore_signal(barrier, inc=1, device_id=device, device_id_type=MESH)

    for k in range(1, n_head):
        greet((s, peer(k)))
    greet((across, h))

    @pl.when(inner[0])
    def _():
        greet((s - INNER, h))
        greet((across - INNER, h))

    @pl.when(inner[1])
    def _():
        greet((s + INNER, h))
        greet((across + INNER, h))

    greetings = n_head + 2 * inner[0].astype(jnp.int32) + 2 * inner[1].astype(jnp.int32)

    starts = (bottom, top)
    ends = (top, bottom)
    steps = (INNER, -INNER)
    gives_all = (y == 0, y == 1)

    def hop(p, c, src):
        return pltpu.make_async_remote_copy(
            src_ref=src.at[p, c], dst_ref=zin.at[p, c], send_sem=zs.at[p, c],
            recv_sem=zr.at[p, c], device_id=(s + steps[p], h), device_id_type=MESH,
        )

    def slant(p, c, src):
        return pltpu.make_async_remote_copy(
            src_ref=src.at[p, c], dst_ref=slant_in.at[p, c - plain], send_sem=rs.at[p, c - plain],
            recv_sem=rr.at[p, c - plain], device_id=(across + steps[p], h), device_id_type=MESH,
        )

    def cross(p, c, src):
        return pltpu.make_async_remote_copy(
            src_ref=src.at[p, c], dst_ref=yin.at[p, c], send_sem=ys.at[p, c],
            recv_sem=yr.at[p, c], device_id=(across, h), device_id_type=MESH,
        )

    def keep(p, i, term):
        for j in range(PARTS):
            own[p, i * PARTS + j] = term[j * rows:(j + 1) * rows]

    def send_first(p, chunk_ids):
        for c in chunk_ids:
            @pl.when(starts[p])
            def _():
                hop(p, c, own).start()
                if c >= plain:
                    slant(p, c, own).start()
                else:
                    @pl.when(gives_all[p])
                    def _():
                        cross(p, c, own).start()

            if c >= plain:
                @pl.when(gives_all[p])
                def _():
                    cross(p, c, own).start()

    def clear(p):
        @pl.when(gives_all[p])
        def _():
            yin[p, plain:chunks] = jnp.zeros((PARTS, rows, HD), F32)

        @pl.when(starts[p])
        def _():
            zin[p] = jnp.zeros(zin.shape[1:], F32)
            slant_in[p] = jnp.zeros(slant_in.shape[1:], F32)

            @pl.when(gives_all[p])
            def _():
                yin[p, 0:plain] = jnp.zeros((plain, rows, HD), F32)

    def carry_on(p):
        @pl.when(jnp.logical_not(starts[p]))
        def _():
            for c in range(chunks):
                hop(p, c, tot).wait_recv()
                tot[p, c] = own[p, c] + zin[p, c]

                @pl.when(jnp.logical_not(ends[p]))
                def _():
                    hop(p, c, tot).start()
                    if c >= plain:
                        slant(p, c, tot).start()

                if c < plain:
                    @pl.when(gives_all[p])
                    def _():
                        cross(p, c, tot).start()

                    @pl.when(jnp.logical_not(gives_all[p]))
                    def _():
                        cross(p, c, zin).start()

    def carried(p, i):
        chunk_ids = range(i * PARTS, (i + 1) * PARTS)
        if chunk_ids[0] < plain:
            @pl.when(jnp.logical_not(starts[p] & gives_all[p]))
            def _():
                for c in chunk_ids:
                    cross(p, c, own).wait_recv()

            pieces = [zin[p, c] + yin[p, c] for c in chunk_ids]
        else:
            @pl.when(jnp.logical_not(gives_all[p]))
            def _():
                for c in chunk_ids:
                    cross(p, c, own).wait_recv()

            @pl.when(jnp.logical_not(starts[p]))
            def _():
                for c in chunk_ids:
                    slant(p, c, own).wait_recv()

            pieces = [zin[p, c] + yin[p, c] + slant_in[p, c - plain] for c in chunk_ids]
        return jnp.concatenate(pieces, axis=0).astype(BF16)

    def drain(p):
        @pl.when(jnp.logical_not(ends[p]))
        def _():
            for c in range(chunks):
                hop(p, c, own).wait_send()
                if c >= plain:
                    slant(p, c, own).wait_send()

        @pl.when(gives_all[p] | jnp.logical_not(starts[p]))
        def _():
            for c in range(plain):
                cross(p, c, own).wait_send()

        @pl.when(gives_all[p])
        def _():
            for c in range(plain, chunks):
                cross(p, c, own).wait_send()

    fetches[0].wait()
    fetches[1].wait()
    for i in range(heads):
        keep(0, i, dot(k_ref[:, cols(i)], v_ref[:, cols(i)], TN))

    pl.semaphore_wait(barrier, greetings)
    send_first(0, range(chunks))
    clear(0)
    clear(1)
    for fetch in fetches[2:]:
        fetch.wait()

    along = jnp.broadcast_to(seg_ref[...], (length, length))
    row_ids = lax.broadcasted_iota(jnp.int32, (length, length), 0)
    col_ids = lax.broadcasted_iota(jnp.int32, (length, length), 1)
    allowed = (along.T == along) & (col_ids <= row_ids)
    for i in range(heads):
        raw = dot(q_ref[:, cols(i)], k_ref[:, cols(i)], NT)
        scores[i] = jnp.where(allowed, raw, 0.0).astype(BF16)
        attn[:, cols(i)] = dot(scores[i], v_ref[:, cols(i)], NN)
        gained[:, cols(i)] = gain_ref[:, cols(i)] * dy_ref[:, cols(i)].astype(F32)
        q_t[i] = q_ref[:, cols(i)].T

    carry_on(0)

    squares = jnp.zeros((length, HD), F32)
    products = jnp.zeros((length, HD), F32)
    for i in range(heads):
        state_b[i] = carried(0, i)
        flat = attn[:, cols(i)] + dot(q_ref[:, cols(i)], state_b[i], NN)
        attn[:, cols(i)] = flat
        squares = squares + flat * flat
        products = products + gained[:, cols(i)] * flat

    norm_out[0:1] = jnp.sum(squares.T, axis=0, keepdims=True)
    norm_out[1:2] = jnp.sum(products.T, axis=0, keepdims=True)
    norm_out[2:8] = jnp.zeros((6, length), F32)

    def share(k):
        return pltpu.make_async_remote_copy(
            src_ref=norm_out, dst_ref=norm_in.at[k - 1], send_sem=ns.at[k - 1],
            recv_sem=nr.at[k - 1], device_id=(s, peer(k)), device_id_type=MESH,
        )

    for k in range(1, n_head):
        share(k).start()
    total = norm_out[...]
    for k in range(1, n_head):
        share(k).wait_recv()
        total = total + norm_in[k - 1]
    inverse_row = lax.rsqrt(total[0:1] / features + 1e-06)
    beta_row = total[1:2] * (inverse_row * inverse_row * inverse_row) / features
    inverse = jnp.broadcast_to(inverse_row, (HD, length)).T
    beta = jnp.broadcast_to(beta_row, (HD, length)).T

    for i in range(heads):
        dattn[i] = (gained[:, cols(i)] * inverse - attn[:, cols(i)] * beta).astype(BF16)
        keep(1, i, dot(q_t[i], dattn[i], NN))
        send_first(1, range(i * PARTS, (i + 1) * PARTS))

    for i in range(heads):
        raw = dot(dattn[i], v_ref[:, cols(i)], NT)
        dscores = jnp.where(allowed, raw, 0.0).astype(BF16)
        gq = dot(dscores, k_ref[:, cols(i)], NN) + dot(dattn[i], state_b[i], NT)
        gq_ref[:, cols(i)] = gq.astype(BF16)
        part_k[i] = dot(dscores, q_ref[:, cols(i)], TN)
        part_v[i] = dot(scores[i], dattn[i], TN)
        out = gain_ref[:, cols(i)] * attn[:, cols(i)] * inverse
        out_ref[:, cols(i)] = out.astype(BF16)

    writes[0].start()
    writes[1].start()

    carry_on(1)

    for i in range(heads):
        later_b = carried(1, i)
        gk = part_k[i] + dot(v_ref[:, cols(i)], later_b, NT)
        gk_ref[:, cols(i)] = gk.astype(BF16)
        gv = part_v[i] + dot(k_ref[:, cols(i)], later_b, NN)
        gv_ref[:, cols(i)] = gv.astype(BF16)

    writes[2].start()
    writes[3].start()
    drain(0)
    drain(1)
    for k in range(1, n_head):
        share(k).wait_send()
    for write in writes:
        write.wait()


def write_out(*refs):
    sources, targets, held, come, go = refs[:4], refs[4:8], refs[8:12], refs[12], refs[13]
    reads = [pltpu.make_async_copy(a, b, come.at[i]) for i, (a, b) in enumerate(zip(sources, held))]
    writes = [pltpu.make_async_copy(a, b, go.at[i]) for i, (a, b) in enumerate(zip(held, targets))]
    for read in reads:
        read.start()
    for read, write in zip(reads, writes):
        read.wait()
        write.start()
    for write in writes:
        write.wait()


def on_device(n_seq, n_head, queries, keys, values, grad_out, gain, segment_ids):
    length, width = queries.shape
    heads = width // HD
    chunks = heads * PARTS
    hbm = pl.BlockSpec(memory_space=pl.ANY)
    states = pltpu.VMEM((2, chunks, HD // PARTS, HD), F32)
    tokens = pltpu.VMEM((length, width), BF16)
    wide = pltpu.VMEM((length, width), F32)
    per_head = pltpu.VMEM((heads, length, HD), F32)
    flags = pltpu.SemaphoreType.DMA((2, chunks))
    results = pl.pallas_call(
        functools.partial(kernel, n_seq, n_head, heads),
        out_shape=[jax.ShapeDtypeStruct((length, width), BF16)] * 4,
        in_specs=[hbm] * 6,
        out_specs=[hbm] * 4,
        scratch_shapes=[tokens] * 4 + [
            tokens,
            tokens,
            tokens,
            tokens,
            pltpu.VMEM((1, width), F32),
            pltpu.VMEM((1, length), jnp.int32),
            states,
            states,
            states,
            states,
            pltpu.VMEM((2, PARTS, HD // PARTS, HD), F32),
            pltpu.VMEM((heads, length, length), BF16),
            pltpu.VMEM((heads, HD, HD), BF16),
            wide,
            wide,
            pltpu.VMEM((heads, HD, length), BF16),
            pltpu.VMEM((heads, length, HD), BF16),
            per_head,
            per_head,
            pltpu.VMEM((8, length), F32),
            pltpu.VMEM((n_head - 1, 8, length), F32),
            pltpu.SemaphoreType.DMA((6,)),
            pltpu.SemaphoreType.DMA((4,)),
            flags,
            flags,
            flags,
            flags,
            pltpu.SemaphoreType.DMA((2, PARTS)),
            pltpu.SemaphoreType.DMA((2, PARTS)),
            pltpu.SemaphoreType.DMA((n_head - 1,)),
            pltpu.SemaphoreType.DMA((n_head - 1,)),
        ],
        compiler_params=pltpu.CompilerParams(
            collective_id=0, has_side_effects=True, vmem_limit_bytes=VMEM,
        ),
    )(queries, keys, values, grad_out, gain.reshape(1, width), segment_ids)
    return pl.pallas_call(
        write_out,
        out_shape=[jax.ShapeDtypeStruct((length, width), BF16)] * 4,
        in_specs=[hbm] * 4,
        out_specs=[hbm] * 4,
        scratch_shapes=[tokens] * 4 + [pltpu.SemaphoreType.DMA((4,))] * 2,
        compiler_params=pltpu.CompilerParams(vmem_limit_bytes=VMEM),
    )(*results)


def solution(mesh):
    sizes = dict(mesh.shape)
    placed = P("seq", "head")
    return jax.shard_map(
        functools.partial(on_device, sizes["seq"], sizes["head"]),
        mesh=mesh,
        in_specs=(placed, placed, placed, placed, P("head"), P("seq", None)),
        out_specs=(placed,) * 4,
        check_vma=False,
    )
```

```python
import functools

import jax
import jax.numpy as jnp
from jax import lax
from jax.experimental import pallas as pl
from jax.experimental.pallas import tpu as pltpu
from jax.sharding import PartitionSpec as P

HD = 128
INNER = 2
PARTS = 2
VMEM = 65000 * 1024
MESH = pl.DeviceIdType.MESH
F32 = jnp.float32
BF16 = jnp.bfloat16


def dot(a, b, dims):
    return lax.dot_general(a, b, (dims, ((), ())), preferred_element_type=F32)


NN = ((1,), (0,))
NT = ((1,), (1,))
TN = ((0,), (0,))


def kernel(
    n_seq, n_head, heads, q_hbm, k_hbm, v_hbm, dy_hbm, gain_hbm, seg_hbm,
    out_hbm, gq_hbm, gk_hbm, gv_hbm,
    out_ref, gq_ref, gk_ref, gv_ref,
    q_ref, k_ref, v_ref, dy_ref, gain_ref, seg_ref,
    own, zin, yin, scores, state_b, attn, gained, q_t, dattn, part_k, part_v,
    norm_out, norm_in, loads, stores, zs, zr, ys, yr, ns, nr,
):
    length = q_ref.shape[0]
    features = n_head * heads * HD
    rows = HD // PARTS
    chunks = heads * PARTS
    s, h = lax.axis_index("seq"), lax.axis_index("head")
    y, z = lax.rem(s, INNER), s // INNER
    depth = n_seq // INNER
    across = s + 1 - 2 * y
    bottom, top = z == 0, z == depth - 1
    inner = jnp.logical_not(bottom), jnp.logical_not(top)

    def cols(i):
        return slice(i * HD, (i + 1) * HD)

    def peer(k):
        return lax.rem(h + k, n_head)

    fetches = [
        pltpu.make_async_copy(src, dst, loads.at[i])
        for i, (src, dst) in enumerate((
            (k_hbm, k_ref), (v_hbm, v_ref), (q_hbm, q_ref), (dy_hbm, dy_ref),
            (gain_hbm, gain_ref), (seg_hbm, seg_ref),
        ))
    ]
    for fetch in fetches:
        fetch.start()
    writes = [
        pltpu.make_async_copy(src, dst, stores.at[i])
        for i, (src, dst) in enumerate((
            (out_ref, out_hbm), (gq_ref, gq_hbm), (gk_ref, gk_hbm), (gv_ref, gv_hbm),
        ))
    ]

    barrier = pltpu.get_barrier_semaphore()

    def greet(device):
        pl.semaphore_signal(barrier, inc=1, device_id=device, device_id_type=MESH)

    for k in range(1, n_head):
        greet((s, peer(k)))
    greet((across, h))

    @pl.when(inner[0])
    def _():
        greet((s - INNER, h))

    @pl.when(inner[1])
    def _():
        greet((s + INNER, h))

    greetings = n_head + inner[0].astype(jnp.int32) + inner[1].astype(jnp.int32)

    starts = (bottom, top)
    ends = (top, bottom)
    nexts = (s + INNER, s - INNER)
    gives_all = (y == 0, y == 1)

    def hop(p, c):
        return pltpu.make_async_remote_copy(
            src_ref=own.at[p, c], dst_ref=zin.at[p, c], send_sem=zs.at[p, c],
            recv_sem=zr.at[p, c], device_id=(nexts[p], h), device_id_type=MESH,
        )

    def cross(p, c, src):
        return pltpu.make_async_remote_copy(
            src_ref=src.at[p, c], dst_ref=yin.at[p, c], send_sem=ys.at[p, c],
            recv_sem=yr.at[p, c], device_id=(across, h), device_id_type=MESH,
        )

    def keep(p, i, term):
        for j in range(PARTS):
            own[p, i * PARTS + j] = term[j * rows:(j + 1) * rows]

    def send_first(p, chunk_ids):
        @pl.when(starts[p])
        def _():
            for c in chunk_ids:
                hop(p, c).start()

                @pl.when(gives_all[p])
                def _():
                    cross(p, c, own).start()

    def clear(p):
        @pl.when(starts[p])
        def _():
            zin[p] = jnp.zeros(zin.shape[1:], F32)

            @pl.when(gives_all[p])
            def _():
                yin[p] = jnp.zeros(yin.shape[1:], F32)

    def carry_on(p):
        @pl.when(jnp.logical_not(starts[p]))
        def _():
            for c in range(chunks):
                hop(p, c).wait_recv()

                own[p, c] = own[p, c] + zin[p, c]

                @pl.when(jnp.logical_not(ends[p]))
                def _():
                    hop(p, c).start()

                @pl.when(gives_all[p])
                def _():
                    cross(p, c, own).start()

                @pl.when(jnp.logical_not(gives_all[p]))
                def _():
                    cross(p, c, zin).start()

    def carried(p, i):
        @pl.when(jnp.logical_not(starts[p] & gives_all[p]))
        def _():
            for j in range(PARTS):
                cross(p, i * PARTS + j, own).wait_recv()

        pieces = [zin[p, i * PARTS + j] + yin[p, i * PARTS + j] for j in range(PARTS)]
        return jnp.concatenate(pieces, axis=0).astype(BF16)

    def drain(p):
        for c in range(chunks):
            @pl.when(jnp.logical_not(ends[p]))
            def _():
                hop(p, c).wait_send()

            @pl.when(gives_all[p] | jnp.logical_not(starts[p]))
            def _():
                cross(p, c, own).wait_send()

    fetches[0].wait()
    fetches[1].wait()
    for i in range(heads):
        keep(0, i, dot(k_ref[:, cols(i)], v_ref[:, cols(i)], TN))

    pl.semaphore_wait(barrier, greetings)
    send_first(0, range(chunks))
    clear(0)
    clear(1)
    for fetch in fetches[2:]:
        fetch.wait()

    along = jnp.broadcast_to(seg_ref[...], (length, length))
    row_ids = lax.broadcasted_iota(jnp.int32, (length, length), 0)
    col_ids = lax.broadcasted_iota(jnp.int32, (length, length), 1)
    allowed = (along.T == along) & (col_ids <= row_ids)
    for i in range(heads):
        raw = dot(q_ref[:, cols(i)], k_ref[:, cols(i)], NT)
        scores[i] = jnp.where(allowed, raw, 0.0).astype(BF16)
        attn[:, cols(i)] = dot(scores[i], v_ref[:, cols(i)], NN)
        gained[:, cols(i)] = gain_ref[:, cols(i)] * dy_ref[:, cols(i)].astype(F32)
        q_t[i] = q_ref[:, cols(i)].T

    carry_on(0)

    squares = jnp.zeros((length, HD), F32)
    products = jnp.zeros((length, HD), F32)
    for i in range(heads):
        state_b[i] = carried(0, i)
        flat = attn[:, cols(i)] + dot(q_ref[:, cols(i)], state_b[i], NN)
        attn[:, cols(i)] = flat
        squares = squares + flat * flat
        products = products + gained[:, cols(i)] * flat

    norm_out[0:1] = jnp.sum(squares.T, axis=0, keepdims=True)
    norm_out[1:2] = jnp.sum(products.T, axis=0, keepdims=True)
    norm_out[2:8] = jnp.zeros((6, length), F32)

    def share(k):
        return pltpu.make_async_remote_copy(
            src_ref=norm_out, dst_ref=norm_in.at[k - 1], send_sem=ns.at[k - 1],
            recv_sem=nr.at[k - 1], device_id=(s, peer(k)), device_id_type=MESH,
        )

    for k in range(1, n_head):
        share(k).start()
    total = norm_out[...]
    for k in range(1, n_head):
        share(k).wait_recv()
        total = total + norm_in[k - 1]
    inverse_row = lax.rsqrt(total[0:1] / features + 1e-06)
    beta_row = total[1:2] * (inverse_row * inverse_row * inverse_row) / features
    inverse = jnp.broadcast_to(inverse_row, (HD, length)).T
    beta = jnp.broadcast_to(beta_row, (HD, length)).T

    for i in range(heads):
        dattn[i] = (gained[:, cols(i)] * inverse - attn[:, cols(i)] * beta).astype(BF16)
        keep(1, i, dot(q_t[i], dattn[i], NN))
        send_first(1, range(i * PARTS, (i + 1) * PARTS))

    for i in range(heads):
        raw = dot(dattn[i], v_ref[:, cols(i)], NT)
        dscores = jnp.where(allowed, raw, 0.0).astype(BF16)
        gq = dot(dscores, k_ref[:, cols(i)], NN) + dot(dattn[i], state_b[i], NT)
        gq_ref[:, cols(i)] = gq.astype(BF16)
        part_k[i] = dot(dscores, q_ref[:, cols(i)], TN)
        part_v[i] = dot(scores[i], dattn[i], TN)
        out = gain_ref[:, cols(i)] * attn[:, cols(i)] * inverse
        out_ref[:, cols(i)] = out.astype(BF16)

    writes[0].start()
    writes[1].start()

    carry_on(1)

    for i in range(heads):
        later_b = carried(1, i)
        gk = part_k[i] + dot(v_ref[:, cols(i)], later_b, NT)
        gk_ref[:, cols(i)] = gk.astype(BF16)
        gv = part_v[i] + dot(k_ref[:, cols(i)], later_b, NN)
        gv_ref[:, cols(i)] = gv.astype(BF16)

    writes[2].start()
    writes[3].start()
    drain(0)
    drain(1)
    for k in range(1, n_head):
        share(k).wait_send()
    for write in writes:
        write.wait()


def write_out(*refs):
    sources, targets, held, come, go = refs[:4], refs[4:8], refs[8:12], refs[12], refs[13]
    reads = [pltpu.make_async_copy(a, b, come.at[i]) for i, (a, b) in enumerate(zip(sources, held))]
    writes = [pltpu.make_async_copy(a, b, go.at[i]) for i, (a, b) in enumerate(zip(held, targets))]
    for read in reads:
        read.start()
    for read, write in zip(reads, writes):
        read.wait()
        write.start()
    for write in writes:
        write.wait()


def on_device(n_seq, n_head, queries, keys, values, grad_out, gain, segment_ids):
    length, width = queries.shape
    heads = width // HD
    chunks = heads * PARTS
    hbm = pl.BlockSpec(memory_space=pl.ANY)
    states = pltpu.VMEM((2, chunks, HD // PARTS, HD), F32)
    tokens = pltpu.VMEM((length, width), BF16)
    wide = pltpu.VMEM((length, width), F32)
    per_head = pltpu.VMEM((heads, length, HD), F32)
    flags = pltpu.SemaphoreType.DMA((2, chunks))
    results = pl.pallas_call(
        functools.partial(kernel, n_seq, n_head, heads),
        out_shape=[jax.ShapeDtypeStruct((length, width), BF16)] * 4,
        in_specs=[hbm] * 6,
        out_specs=[hbm] * 4,
        scratch_shapes=[tokens] * 4 + [
            tokens,
            tokens,
            tokens,
            tokens,
            pltpu.VMEM((1, width), F32),
            pltpu.VMEM((1, length), jnp.int32),
            states,
            states,
            states,
            pltpu.VMEM((heads, length, length), BF16),
            pltpu.VMEM((heads, HD, HD), BF16),
            wide,
            wide,
            pltpu.VMEM((heads, HD, length), BF16),
            pltpu.VMEM((heads, length, HD), BF16),
            per_head,
            per_head,
            pltpu.VMEM((8, length), F32),
            pltpu.VMEM((n_head - 1, 8, length), F32),
            pltpu.SemaphoreType.DMA((6,)),
            pltpu.SemaphoreType.DMA((4,)),
            flags,
            flags,
            flags,
            flags,
            pltpu.SemaphoreType.DMA((n_head - 1,)),
            pltpu.SemaphoreType.DMA((n_head - 1,)),
        ],
        compiler_params=pltpu.CompilerParams(
            collective_id=0, has_side_effects=True, vmem_limit_bytes=VMEM,
        ),
    )(queries, keys, values, grad_out, gain.reshape(1, width), segment_ids)
    return pl.pallas_call(
        write_out,
        out_shape=[jax.ShapeDtypeStruct((length, width), BF16)] * 4,
        in_specs=[hbm] * 4,
        out_specs=[hbm] * 4,
        scratch_shapes=[tokens] * 4 + [pltpu.SemaphoreType.DMA((4,))] * 2,
        compiler_params=pltpu.CompilerParams(vmem_limit_bytes=VMEM),
    )(*results)


def solution(mesh):
    sizes = dict(mesh.shape)
    placed = P("seq", "head")
    return jax.shard_map(
        functools.partial(on_device, sizes["seq"], sizes["head"]),
        mesh=mesh,
        in_specs=(placed, placed, placed, placed, P("head"), P("seq", None)),
        out_specs=(placed,) * 4,
        check_vma=False,
    )
```
